1024 devices in a mesh: dp: 128 (over y_lo, z, core), tensor: 8 (over y_hi, x).
Axes of the slice: x: 4, y: 4 (y_hi: 2, y_lo: 2; y = y_hi * 2 + y_lo), z: 32, core: 2. Of those that a mesh axis runs over, the one named last changes fastest.
Arguments:
- teacher_down: bfloat16 [4096, 28672], P('dp', 'tensor'), may hold values from -0.125 to 0.125
- kept_blocks: int32 [16], replicated, may hold values from 0 to 223, as said below
- block_slot: int32 [16], replicated, may hold values from 0 to 15, as said below
- hidden: bfloat16 [24576, 2048], P('dp', 'tensor'), may hold values from -6 to 6
- target: bfloat16 [24576, 4096], P('dp'), may hold values from -24 to 24
Outputs:
- student_out: bfloat16 [24576, 4096], P('dp', 'tensor')
- grad_down: float32 [4096, 2048], P('dp', 'tensor')
The draws below stay inside these ranges and needn't reach their ends.
Inputs may be any that keep to these rules, and one draw needn't show every extreme that they name: `kept_blocks`: distinct teacher blocks; no teacher shard (blocks b with one value of b // 28) holds more than 4 of them, and some shard holds exactly 4. `block_slot`: each of 0 to 15 exactly once; student block s belongs to holder s // 2; at most 2 blocks of one teacher shard go to one holder, and in every draw some holder receives 2 blocks from one teacher shard.
All inputs are finite; a program needn't handle non-finite values.
Results may differ from the reference program's by a relative error of at most 0.017.
Values may be sent and summed in bfloat16 or wider, within the bound.
No kernel may reach another device: no remote copies, remote signals or barrier semaphores. Data moves between devices by JAX's collectives and lax.ppermute only.
A program may use at most 32 MiB of HBM per device.

```python
import math
import jax
import jax.numpy as jnp
from jax import lax

FF = 28672
DW = 4096
BLK = 128
KEPT = 16
SRC_MOST = 4
TOKENS = 24576
N_TENSOR = 8


def kept_and_slots(key):
    shard_blocks = FF // BLK // N_TENSOR
    own_blocks = KEPT // N_TENSOR
    first_count = min(own_blocks, SRC_MOST)
    subkeys = jax.random.split(key, 6)
    shard_order = jax.random.permutation(subkeys[0], N_TENSOR).astype(jnp.int32)
    spare_slots = jax.random.permutation(subkeys[1], (N_TENSOR - 1) * SRC_MOST)[:KEPT - SRC_MOST].astype(jnp.int32)
    shard_of = jnp.concatenate([jnp.full((SRC_MOST,), shard_order[0], jnp.int32), shard_order[1 + spare_slots // SRC_MOST]])
    place_in = jnp.concatenate([jnp.arange(SRC_MOST, dtype=jnp.int32), spare_slots % SRC_MOST])
    offsets = jax.random.permutation(subkeys[2], shard_blocks)[:SRC_MOST].astype(jnp.int32)
    within = (offsets[place_in] + shard_of * 5) % shard_blocks
    chosen = shard_of * shard_blocks + within
    start_owner = jax.random.randint(subkeys[3], (), 0, N_TENSOR).astype(jnp.int32)
    remaining = jax.random.permutation(subkeys[4], KEPT - first_count).astype(jnp.int32)
    slot_list = jnp.concatenate([start_owner * own_blocks + jnp.arange(first_count, dtype=jnp.int32), (start_owner * own_blocks + first_count + remaining) % KEPT])
    shuffle = jax.random.permutation(subkeys[5], KEPT)
    return (chosen[shuffle].astype(jnp.int32), slot_list[shuffle].astype(jnp.int32))


def draw_kept_blocks(key, part):
    shared = kept_and_slots(key)
    return shared[0]


def draw_block_slot(key, part):
    shared = kept_and_slots(key)
    return shared[1]


def strengthened(result, own_key, source, target, parts, factor):
    def block_of(dim):
        return (jnp.arange(result.shape[dim]) // (result.shape[dim] // parts)).reshape((-1,) + (1,) * (result.ndim - 1 - dim))

    first = jax.random.permutation(own_key, parts)[block_of(target)]
    far = (block_of(target) + parts // 2) % parts
    return jnp.where((block_of(source) == first) | (block_of(source) == far), factor * result, result)


def shard_levels(own_key, dims, cuts, smallest, largest):
    def one(position, shards_of):
        steps = jax.random.uniform(jax.random.fold_in(jax.random.fold_in(own_key, 6), position), (shards_of,), jnp.float32, smallest / len(cuts), largest / len(cuts))
        return jnp.repeat(jnp.exp(steps), dims[position] // shards_of).reshape((-1,) + (1,) * (len(dims) - position - 1))

    factor_of = one(*cuts[0])
    for cut in cuts[1:]:
        factor_of = factor_of * one(*cut)
    return factor_of


def normal_values(stream_key, dims, deviation, bound, shards=(), kind=jnp.bfloat16):
    values = deviation * jax.random.normal(stream_key, dims, jnp.float32)
    if shards:
        values = values * shard_levels(stream_key, dims, shards, -0.22, 0.18)
    return jnp.clip(values, -bound, bound).astype(kind)


def heavy_noise(stream_key, dims, scale, bound, shards, heavy, kind=jnp.bfloat16):
    drawn = scale * jax.random.normal(stream_key, dims, jnp.float32)
    if shards:
        drawn = drawn * shard_levels(stream_key, dims, shards, -0.22, 0.18)
    return jnp.clip(strengthened(drawn, jax.random.fold_in(stream_key, 3), *heavy), -bound, bound).astype(kind)


def setup_inputs(seed: int = 0) -> dict:
    splits = jax.random.split(jax.random.key(seed), 6)
    return {
        "teacher_down": normal_values(splits[0], (DW, FF), (KEPT * BLK) ** -0.5, 0.125, ((0, 128), (1, 8))),
        "kept_blocks": draw_kept_blocks(jax.random.fold_in(splits[5], 71), 0),
        "block_slot": draw_block_slot(jax.random.fold_in(splits[5], 71), 0),
        "hidden": normal_values(splits[3], (TOKENS, KEPT * BLK), 1.0, 6.0, ((0, 128), (1, 8))),
        "target": heavy_noise(splits[4], (TOKENS, DW), 1.0, 24.0, ((0, 128),), (0, 1, 128, 5.5)),
    }


def reference(teacher_down, kept_blocks, block_slot, hidden, target):
    blocks = teacher_down.reshape(DW, FF // BLK, BLK)
    picked = jnp.take(blocks, kept_blocks.astype(jnp.int32), axis=1)
    student = jnp.zeros((DW, KEPT, BLK), teacher_down.dtype).at[:, block_slot.astype(jnp.int32)].set(picked)
    student = student.reshape(DW, KEPT * BLK)
    span_units = KEPT * BLK // N_TENSOR
    summed = jnp.zeros((hidden.shape[0], DW), jnp.float32)
    for holder in range(N_TENSOR):
        product = lax.dot_general(hidden[:, holder * span_units:(holder + 1) * span_units], student[:, holder * span_units:(holder + 1) * span_units], (((1,), (1,)), ((), ())), preferred_element_type=jnp.float32)
        rounded = lax.optimization_barrier(product.astype(jnp.bfloat16))
        summed = summed + rounded.astype(jnp.float32)
    student_out = summed.astype(jnp.bfloat16)
    residue = (student_out.astype(jnp.float32) - target.astype(jnp.float32)).astype(jnp.bfloat16)
    gradient = lax.dot_general(residue, hidden, (((0,), (0,)), ((), ())), preferred_element_type=jnp.float32)
    gradient = gradient * (1.0 / math.sqrt(TOKENS))
    return (student_out, gradient)
```

```python
import math

import jax
import jax.numpy as jnp
import numpy as np
from jax import lax
from jax.experimental import pallas as pl
from jax.experimental.pallas import tpu as pltpu
from jax.sharding import Mesh
from jax.sharding import PartitionSpec as P

BF16 = jnp.bfloat16
F32 = jnp.float32
I32 = jnp.int32

AXES = ("ylo", "zh", "zl", "core", "yhi", "x")
SIZES = (2, 8, 4, 2, 2, 4)
TENSOR = ("yhi", "x")
PLANE = ("ylo", "yhi", "x")
PAIR = ("ylo", "core")

BLK = 128
KEPT = 16
MOST = 4
NT = 8
NH = 8
NL = 4
R = 4
SHARD = 28
TOK = 192
UNITS = 256

VMEM = pl.BlockSpec(memory_space=pltpu.VMEM)
SMEM = pl.BlockSpec(memory_space=pltpu.SMEM)
PARAMS = pltpu.CompilerParams(vmem_limit_bytes=40 * 1024 * 1024)


def iota(shape, axis):
    return lax.broadcasted_iota(I32, shape, axis)


def onehot(mask):
    return jnp.where(mask, 1.0, 0.0).astype(BF16)


def call(kernel, out, specs, *args):
    return pl.pallas_call(
        kernel,
        out_shape=out,
        in_specs=specs,
        out_specs=jax.tree.map(lambda _: VMEM, out),
        compiler_params=PARAMS,
    )(*args)


def pack_kernel(kept, me, teacher, packed):
    base = me[0] * SHARD
    count = jnp.int32(0)
    places = [jnp.int32(0)] * MOST
    for j in range(KEPT):
        within = kept[j] - base
        mine = (within >= 0) & (within < SHARD)
        for p in range(MOST):
            places[p] = jnp.where(mine & (count == p), within, places[p])
        count = count + mine.astype(I32)
    rows = NT * R
    picked = jnp.concatenate(
        [teacher[:, pl.ds(pl.multiple_of(w * BLK, BLK), BLK)] for w in places], axis=0
    )
    n = MOST * rows
    o, i = iota((n, n), 0), iota((n, n), 1)
    t, p, r = o // (MOST * R), (o // R) % MOST, o % R
    order = onehot(i == p * rows + t * R + r)
    packed[...] = jnp.dot(order, picked, preferred_element_type=F32).astype(BF16)


def compact_kernel(kept, slot, arrived, piece):
    n, m = KEPT * R, NT * MOST * R
    o, i = iota((n, m), 0), iota((n, m), 1)
    shard = [(kept[j] * 2341) >> 16 for j in range(KEPT)]
    wanted = jnp.zeros((n, m), I32)
    for j in range(KEPT):
        place = jnp.int32(0)
        for k in range(j):
            place = place + (shard[k] == shard[j]).astype(I32)
        wanted = jnp.where(o // R == slot[j], (shard[j] * MOST + place) * R, wanted)
    order = onehot(i == wanted + o % R)
    rows = jnp.dot(order, arrived[...], preferred_element_type=F32).astype(BF16)
    for h in range(NH):
        piece[h] = rows


def regroup_kernel(pieces, grouped):
    x = pieces[...].astype(F32)
    rows = jnp.concatenate(
        [
            x[h, s * R : (s + 1) * R]
            for s in range(KEPT)
            for h in range(NH)
        ],
        axis=0,
    ).astype(BF16)
    for k in range(NL):
        grouped[k] = rows


def target_kernel(me, target, chosen):
    half = target.shape[1] // 2
    n = 2 * NH * NL * R
    k, j = iota((half, n), 0), iota((half, n), 1)
    core, low, high, r = j // 128, (j // 32) % NL, (j // R) % NH, j % R
    column = (high * NL + low) * 64 + core * 32 + me[0] * R + r
    order = onehot(k == column)
    for y in range(2):
        got = jnp.dot(
            target[:, y * half : (y + 1) * half], order, preferred_element_type=F32
        ).astype(BF16)
        for c in range(2):
            chosen[2 * y + c] = got[:, c * 128 : (c + 1) * 128]


def main_kernel(core, own, other, weights, target, out, gradient, full):
    c = core[0]
    for k in range(NL):
        for s in range(KEPT):
            full[k * 32 : (k + 1) * 32, s * BLK : (s + 1) * BLK] = weights[
                k, s * 32 : (s + 1) * 32, :
            ]
    residue = []
    for y in range(2):
        for rel, hidden in ((0, own), (1, other)):
            group = 2 * y + (c if rel == 0 else 1 - c)
            total = jnp.zeros((TOK, 128), F32)
            for t in range(NT):
                total = total + lax.dot_general(
                    hidden[y * NT + t],
                    full[:, t * UNITS : (t + 1) * UNITS],
                    (((1,), (1,)), ((), ())),
                    preferred_element_type=F32,
                )
            rounded = total.astype(BF16)
            out[group] = rounded
            residue.append(
                (rounded.astype(F32) - target[group].astype(F32)).astype(BF16)
            )
    for t in range(NT):
        total = jnp.zeros((128, UNITS), F32)
        for y in range(2):
            for rel, hidden in ((0, own), (1, other)):
                total = total + lax.dot_general(
                    residue[2 * y + rel],
                    hidden[y * NT + t],
                    (((0,), (0,)), ((), ())),
                    preferred_element_type=F32,
                )
        total = total.astype(BF16)
        for k in range(NL):
            for s in range(2):
                gradient[k, (2 * t + s) * 32 : (2 * t + s + 1) * 32, :] = total[
                    k * 32 : (k + 1) * 32, s * BLK : (s + 1) * BLK
                ]


def first_sum_kernel(parts, summed):
    total = parts[0].astype(F32)
    for k in range(1, NL):
        total = total + parts[k].astype(F32)
    for h in range(NH):
        summed[h] = jnp.concatenate(
            [total[s * 32 + h * R : s * 32 + (h + 1) * R] for s in range(KEPT)], axis=0
        ).astype(BF16)


def second_sum_kernel(parts, summed):
    total = parts[0].astype(F32)
    for k in range(1, NH):
        total = total + parts[k].astype(F32)
    for u in range(NT):
        summed[u] = total[u * 8 : (u + 1) * 8]


def last_kernel(factor, parts, gradient):
    for t in range(NT):
        rows = parts[t] * factor
        for s in range(2):
            gradient[t * R : (t + 1) * R, s * BLK : (s + 1) * BLK] = rows[
                s * R : (s + 1) * R
            ]


def spread_kernel(parts, blocks):
    k, j = iota((512, 512), 0), iota((512, 512), 1)
    x, half, core, odd, low, r = (
        j // 128,
        (j // 64) % 2,
        (j // 32) % 2,
        (j // 16) % 2,
        (j // R) % NL,
        j % R,
    )
    order = onehot(k == (half * 2 + core) * 128 + low * 32 + (2 * x + odd) * R + r)
    for y in range(2):
        rows = jnp.concatenate(
            [
                parts[2 * y + c, h * 96 : (h + 1) * 96, :]
                for h in range(2)
                for c in range(2)
            ],
            axis=1,
        )
        got = jnp.dot(rows, order, preferred_element_type=F32).astype(BF16)
        for i in range(4):
            blocks[4 * y + i] = got[:, i * 128 : (i + 1) * 128]


def gather_kernel(parts, out):
    rows = jnp.concatenate([parts[t] for t in range(NT)], axis=1)
    k, j = iota((1024, 512), 0), iota((1024, 512), 1)
    z, core, t, r = j // 64, (j // 32) % 2, (j // R) % NT, j % R
    lane = t * 128 + core * 32 + z * R + r
    for half in range(2):
        order = onehot(k == lane + half * 64)
        out[half * 96 : (half + 1) * 96, :] = jnp.dot(
            rows, order, preferred_element_type=F32
        ).astype(BF16)


def exchange(x, axes):
    return lax.all_to_all(x, axes, 0, 0)


def body(teacher, kept, slot, hidden, target):
    me = lax.axis_index(TENSOR).astype(I32)[None]
    core = lax.axis_index("core").astype(I32)[None]
    shape = jax.ShapeDtypeStruct

    packed = call(pack_kernel, shape((128, 128), BF16), [SMEM, SMEM, VMEM], kept, me, teacher)
    arrived = exchange(packed.reshape(NT, 16, 128), TENSOR)

    plane = exchange(jnp.broadcast_to(hidden[None], (16,) + hidden.shape), PLANE)
    chosen = call(target_kernel, shape((4, TOK, 128), BF16), [SMEM, VMEM], me, target)
    wanted = exchange(chosen, PAIR)

    piece = call(
        compact_kernel,
        shape((NH, 64, 128), BF16),
        [SMEM, SMEM, VMEM],
        kept,
        slot,
        arrived.reshape(128, 128),
    )
    pieces = exchange(piece, "zh")
    grouped = call(regroup_kernel, shape((NL, 512, 128), BF16), [VMEM], pieces)
    weights = exchange(grouped, "zl")
    swap = [(0, 1), (1, 0)]
    other = lax.ppermute(plane, "core", swap)

    out, gradient = pl.pallas_call(
        main_kernel,
        out_shape=(shape((4, TOK, 128), BF16), shape((NL, 512, 128), BF16)),
        in_specs=[SMEM, VMEM, VMEM, VMEM, VMEM],
        out_specs=(VMEM, VMEM),
        scratch_shapes=[pltpu.VMEM((128, KEPT * BLK), BF16)],
        compiler_params=PARAMS,
    )(core, plane, other, weights, wanted)

    parts = exchange(gradient, "zl")
    summed = call(first_sum_kernel, shape((NH, 64, 128), BF16), [VMEM], parts)
    parts = exchange(summed, "zh")
    summed = call(second_sum_kernel, shape((NT, 8, 128), F32), [VMEM], parts)
    parts = exchange(summed, TENSOR)
    factor = 1.0 / math.sqrt(TOK * 128)
    grad = call(
        lambda a, b: last_kernel(factor, a, b), shape((32, UNITS), F32), [VMEM], parts
    )

    groups = exchange(out, PAIR)
    blocks = call(spread_kernel, shape((NT, 96, 128), BF16), [VMEM], groups)
    blocks = exchange(blocks, TENSOR)
    student = call(gather_kernel, shape((TOK, 512), BF16), [VMEM], blocks)
    return student, grad


def solution(mesh):
    fine = Mesh(np.asarray(mesh.devices).reshape(SIZES), AXES)
    dp = ("ylo", "zh", "zl", "core")
    placed = (P(dp, TENSOR), P(), P(), P(dp, TENSOR), P(dp, None))
    return jax.shard_map(
        body,
        mesh=fine,
        in_specs=placed,
        out_specs=(P(dp, TENSOR), P(dp, TENSOR)),
        check_vma=False,
    )
```

```python
import math

import jax
import jax.numpy as jnp
import numpy as np
from jax import lax
from jax.experimental import pallas as pl
from jax.experimental.pallas import tpu as pltpu
from jax.sharding import Mesh
from jax.sharding import PartitionSpec as P

BF16 = jnp.bfloat16
F32 = jnp.float32
I32 = jnp.int32

AXES = ("ylo", "zh", "zl", "core", "yhi", "x")
SIZES = (2, 8, 4, 2, 2, 4)
TENSOR = ("yhi", "x")
PLANE = ("ylo", "yhi", "x")
PAIR = ("ylo", "core")

BLK = 128
KEPT = 16
MOST = 4
NT = 8
NH = 8
NL = 4
R = 4
SHARD = 28
TOK = 192
UNITS = 256

VMEM = pl.BlockSpec(memory_space=pltpu.VMEM)
SMEM = pl.BlockSpec(memory_space=pltpu.SMEM)
PARAMS = pltpu.CompilerParams(vmem_limit_bytes=40 * 1024 * 1024)


def iota(shape, axis):
    return lax.broadcasted_iota(I32, shape, axis)


def onehot(mask):
    return jnp.where(mask, 1.0, 0.0).astype(BF16)


def call(kernel, out, specs, *args):
    return pl.pallas_call(
        kernel,
        out_shape=out,
        in_specs=specs,
        out_specs=jax.tree.map(lambda _: VMEM, out),
        compiler_params=PARAMS,
    )(*args)


def pack_kernel(kept, me, teacher, hidden, packed):
    base = me[0] * SHARD
    count = jnp.int32(0)
    places = [jnp.int32(0)] * MOST
    for j in range(KEPT):
        within = kept[j] - base
        mine = (within >= 0) & (within < SHARD)
        for p in range(MOST):
            places[p] = jnp.where(mine & (count == p), within, places[p])
        count = count + mine.astype(I32)
    rows = NT * R
    picked = jnp.concatenate(
        [teacher[:, pl.ds(pl.multiple_of(w * BLK, BLK), BLK)] for w in places], axis=0
    )
    n = MOST * rows
    o, i = iota((n, n), 0), iota((n, n), 1)
    t, p, r = o // (MOST * R), (o // R) % MOST, o % R
    order = onehot(i == p * rows + t * R + r)
    blocks = jnp.dot(order, picked, preferred_element_type=F32).astype(BF16)
    for m in range(2 * NT):
        packed[m, :TOK] = hidden[:, :BLK]
        packed[m, TOK : 2 * TOK] = hidden[:, BLK:]
        packed[m, 2 * TOK :] = blocks[(m % NT) * 16 : (m % NT + 1) * 16]


def compact_kernel(ylo, kept, slot, arrived, piece):
    n, m = KEPT * R, NT * MOST * R
    o, i = iota((n, m), 0), iota((n, m), 1)
    shard = [(kept[j] * 2341) >> 16 for j in range(KEPT)]
    wanted = jnp.zeros((n, m), I32)
    for j in range(KEPT):
        place = jnp.int32(0)
        for k in range(j):
            place = place + (shard[k] == shard[j]).astype(I32)
        wanted = jnp.where(o // R == slot[j], (shard[j] * MOST + place) * R, wanted)
    order = onehot(i == wanted + o % R)
    sent = jnp.concatenate([arrived[u] for u in range(NT)], axis=0)
    rows = jnp.dot(order, sent, preferred_element_type=F32).astype(BF16)
    for h in range(NH):
        piece[h] = rows


def regroup_kernel(pieces, grouped):
    x = pieces[...].astype(F32)
    rows = jnp.concatenate(
        [x[h, s * R : (s + 1) * R] for s in range(KEPT) for h in range(NH)], axis=0
    ).astype(BF16)
    for k in range(NL):
        grouped[k] = rows


def target_kernel(ylo, mine, me, target, *chosen):
    half = target.shape[1] // 2
    n = 2 * NH * NL * R
    k, j = iota((half, n), 0), iota((half, n), 1)
    core, low, high, r = j // 128, (j // 32) % NL, (j // R) % NH, j % R
    column = (high * NL + low) * 64 + (core ^ mine[0]) * 32 + me[0] * R + r
    order = onehot(k == column)
    for dy in range(2):
        start = pl.multiple_of((ylo[0] ^ dy) * half, half)
        got = jnp.dot(
            target[:, pl.ds(start, half)], order, preferred_element_type=F32
        ).astype(BF16)
        for dc in range(2):
            chosen[2 * dy + dc][...] = got[:, dc * 128 : (dc + 1) * 128]


def main_kernel(ylo, own, other, weights, t0, t1, t2, t3, o0, o1, o2, o3, gradient, full):
    for k in range(NL):
        for s in range(KEPT):
            full[k * 32 : (k + 1) * 32, s * BLK : (s + 1) * BLK] = weights[
                k, s * 32 : (s + 1) * 32, :
            ]
    targets, outs = (t0, t1, t2, t3), (o0, o1, o2, o3)

    def tokens(dy, dc, t):
        block = ((own, other)[dc]).at[(ylo[0] ^ dy) * NT + t]
        return jnp.concatenate([block[:TOK], block[TOK : 2 * TOK]], axis=1)

    residue = []
    for dy in range(2):
        for dc in range(2):
            total = jnp.zeros((TOK, 128), F32)
            for t in range(NT):
                total = total + lax.dot_general(
                    tokens(dy, dc, t),
                    full[:, t * UNITS : (t + 1) * UNITS],
                    (((1,), (1,)), ((), ())),
                    preferred_element_type=F32,
                )
            rounded = total.astype(BF16)
            outs[2 * dy + dc][...] = rounded
            wanted = targets[2 * dy + dc][...]
            residue.append((rounded.astype(F32) - wanted.astype(F32)).astype(BF16))
    for t in range(NT):
        total = jnp.zeros((128, UNITS), F32)
        for dy in range(2):
            for dc in range(2):
                total = total + lax.dot_general(
                    residue[2 * dy + dc],
                    tokens(dy, dc, t),
                    (((0,), (0,)), ((), ())),
                    preferred_element_type=F32,
                )
        total = total.astype(BF16)
        for k in range(NL):
            for s in range(2):
                gradient[k, (2 * t + s) * 32 : (2 * t + s + 1) * 32, :] = total[
                    k * 32 : (k + 1) * 32, s * BLK : (s + 1) * BLK
                ]


def first_sum_kernel(parts, summed):
    total = parts[0].astype(F32)
    for k in range(1, NL):
        total = total + parts[k].astype(F32)
    for h in range(NH):
        summed[h] = jnp.concatenate(
            [total[s * 32 + h * R : s * 32 + (h + 1) * R] for s in range(KEPT)], axis=0
        ).astype(BF16)


def spread_kernel(ylo, mine, p0, p1, p2, p3, blocks):
    parts = (p0, p1, p2, p3)
    k, j = iota((512, 512), 0), iota((512, 512), 1)
    x, half, core, odd, low, r = (
        j // 128,
        (j // 64) % 2,
        (j // 32) % 2,
        (j // 16) % 2,
        (j // R) % NL,
        j % R,
    )
    column = low * 32 + (2 * x + odd) * R + r
    order = onehot(k == (half * 2 + (core ^ mine[0])) * 128 + column)
    for dy in range(2):
        rows = jnp.concatenate(
            [
                parts[2 * dy + dc][h * 96 : (h + 1) * 96, :]
                for h in range(2)
                for dc in range(2)
            ],
            axis=1,
        )
        got = jnp.dot(rows, order, preferred_element_type=F32).astype(BF16)
        for i in range(4):
            blocks[4 * (ylo[0] ^ dy) + i] = got[:, i * 128 : (i + 1) * 128]


def second_sum_kernel(parts, blocks, joined):
    total = parts[0].astype(F32)
    for k in range(1, NH):
        total = total + parts[k].astype(F32)
    high = total.astype(BF16).astype(F32)
    low = total - high
    for u in range(NT):
        rows = slice(u * 8, (u + 1) * 8)
        joined[u, :96] = blocks[u]
        joined[u, 96:] = jnp.concatenate([high[rows], low[rows]], axis=0).astype(BF16)


def last_kernel(factor, parts, out, gradient):
    for t in range(NT):
        both = parts[t, 96:].astype(F32)
        rows = (both[:8] + both[8:]) * factor
        for s in range(2):
            gradient[t * R : (t + 1) * R, s * BLK : (s + 1) * BLK] = rows[
                s * R : (s + 1) * R
            ]
    rows = jnp.concatenate([parts[t, :96] for t in range(NT)], axis=1)
    k, j = iota((1024, 512), 0), iota((1024, 512), 1)
    z, core, t, r = j // 64, (j // 32) % 2, (j // R) % NT, j % R
    lane = t * 128 + core * 32 + z * R + r
    for half in range(2):
        order = onehot(k == lane + half * 64)
        out[half * 96 : (half + 1) * 96, :] = jnp.dot(
            rows, order, preferred_element_type=F32
        ).astype(BF16)


def exchange(x, axes):
    return lax.all_to_all(x, axes, 0, 0)


def swap(x, dy, dc):
    axes = ("ylo", "core")
    perm = [(2 * y + c, 2 * (y ^ dy) + (c ^ dc)) for y in range(2) for c in range(2)]
    return lax.ppermute(x, axes, perm)


def pairs(own, *others):
    return [own] + [swap(x, i // 2, i % 2) for i, x in enumerate(others, 1)]


def body(teacher, kept, slot, hidden, target):
    place = [lax.axis_index(a).astype(I32)[None] for a in ("ylo", "core", TENSOR)]
    shape = jax.ShapeDtypeStruct
    tile = shape((TOK, 128), BF16)

    packed = call(
        pack_kernel,
        shape((16, 400, 128), BF16),
        [SMEM, SMEM, VMEM, VMEM],
        kept,
        place[2],
        teacher,
        hidden,
    )
    plane = exchange(packed, PLANE)
    chosen = call(target_kernel, (tile,) * 4, [SMEM] * 3 + [VMEM], *place, target)

    smem = pl.BlockSpec(memory_space=pltpu.SMEM)
    plane, *chosen = lax.optimization_barrier((plane, *chosen))
    piece = pl.pallas_call(
        compact_kernel,
        out_shape=shape((NH, 64, 128), BF16),
        grid_spec=pltpu.PrefetchScalarGridSpec(
            num_scalar_prefetch=1,
            grid=(1,),
            in_specs=[smem, smem, pl.BlockSpec((NT, 16, 128), lambda i, y: (y[0], 24, 0))],
            out_specs=pl.BlockSpec((NH, 64, 128), lambda i, y: (0, 0, 0)),
        ),
        compiler_params=PARAMS,
    )(place[0], kept, slot, plane)
    pieces = exchange(piece, "zh")
    other = swap(plane, 0, 1)
    wanted = pairs(*chosen)
    pieces, other, *wanted = lax.optimization_barrier((pieces, other, *wanted))
    grouped = call(regroup_kernel, shape((NL, 512, 128), BF16), [VMEM], pieces)
    weights = exchange(grouped, "zl")

    *outs, gradient = pl.pallas_call(
        main_kernel,
        out_shape=(tile,) * 4 + (shape((NL, 512, 128), BF16),),
        in_specs=[SMEM] + [VMEM] * 7,
        out_specs=(VMEM,) * 5,
        scratch_shapes=[pltpu.VMEM((128, KEPT * BLK), BF16)],
        compiler_params=PARAMS,
    )(place[0], plane, other, weights, *wanted)

    parts = exchange(gradient, "zl")
    summed = call(first_sum_kernel, shape((NH, 64, 128), BF16), [VMEM], parts)
    parts = exchange(summed, "zh")
    groups = pairs(*outs)
    blocks = call(
        spread_kernel, shape((NT, 96, 128), BF16), [SMEM] * 2 + [VMEM] * 4, *place[:2], *groups
    )
    joined = call(
        second_sum_kernel, shape((NT, 112, 128), BF16), [VMEM, VMEM], parts, blocks
    )
    parts = exchange(joined, TENSOR)
    factor = 1.0 / math.sqrt(TOK * 128)
    student, grad = call(
        lambda *refs: last_kernel(factor, *refs),
        (shape((TOK, 512), BF16), shape((32, UNITS), F32)),
        [VMEM],
        parts,
    )
    return student, grad


def solution(mesh):
    fine = Mesh(np.asarray(mesh.devices).reshape(SIZES), AXES)
    dp = ("ylo", "zh", "zl", "core")
    placed = (P(dp, TENSOR), P(), P(), P(dp, TENSOR), P(dp, None))
    return jax.shard_map(
        body,
        mesh=fine,
        in_specs=placed,
        out_specs=(P(dp, TENSOR), P(dp, TENSOR)),
        check_vma=False,
    )
```

```python
import math

import jax
import jax.numpy as jnp
import numpy as np
from jax import lax
from jax.experimental import pallas as pl
from jax.experimental.pallas import tpu as pltpu
from jax.sharding import Mesh
from jax.sharding import PartitionSpec as P

BF16 = jnp.bfloat16
F32 = jnp.float32
I32 = jnp.int32

AXES = ("ylo", "zh", "zl", "core", "yhi", "x")
SIZES = (2, 8, 4, 2, 2, 4)
TENSOR = ("yhi", "x")

BLK = 128
KEPT = 16
MOST = 4
NT = 8
NH = 8
NL = 4
ORDER = tuple((h + NH // 2) % NH for h in range(NH))
R = 4
SHARD = 28
TOK = 192
UNITS = 256

VMEM = pl.BlockSpec(memory_space=pltpu.VMEM)
SMEM = pl.BlockSpec(memory_space=pltpu.SMEM)
PARAMS = pltpu.CompilerParams(vmem_limit_bytes=40 * 1024 * 1024)


def iota(shape, axis):
    return lax.broadcasted_iota(I32, shape, axis)


def onehot(mask):
    return jnp.where(mask, 1.0, 0.0).astype(BF16)


def call(kernel, out, specs, *args):
    return pl.pallas_call(
        kernel,
        out_shape=out,
        in_specs=specs,
        out_specs=jax.tree.map(lambda _: VMEM, out),
        compiler_params=PARAMS,
    )(*args)


def pack_kernel(kept, me, teacher, hidden, packed):
    base = me[0] * SHARD
    count = jnp.int32(0)
    places = [jnp.int32(0)] * MOST
    for j in range(KEPT):
        within = kept[j] - base
        mine = (within >= 0) & (within < SHARD)
        for p in range(MOST):
            places[p] = jnp.where(mine & (count == p), within, places[p])
        count = count + mine.astype(I32)
    rows = NT * R
    picked = jnp.concatenate(
        [teacher[:, pl.ds(pl.multiple_of(w * BLK, BLK), BLK)] for w in places], axis=0
    )
    n = MOST * rows
    o, i = iota((n, n), 0), iota((n, n), 1)
    t, p, r = o // (MOST * R), (o // R) % MOST, o % R
    order = onehot(i == p * rows + t * R + r)
    blocks = jnp.dot(order, picked, preferred_element_type=F32).astype(BF16)
    for m in range(NT):
        packed[m, :TOK] = hidden[:, :BLK]
        packed[m, TOK : 2 * TOK] = hidden[:, BLK:]
        packed[m, 2 * TOK :] = blocks[m * 16 : (m + 1) * 16]


def compact_kernel(kept, slot, arrived, piece):
    n, m = KEPT * R, NT * MOST * R
    o, i = iota((n, m), 0), iota((n, m), 1)
    shard = [(kept[j] * 2341) >> 16 for j in range(KEPT)]
    wanted = jnp.zeros((n, m), I32)
    for j in range(KEPT):
        place = jnp.int32(0)
        for k in range(j):
            place = place + (shard[k] == shard[j]).astype(I32)
        wanted = jnp.where(o // R == slot[j], (shard[j] * MOST + place) * R, wanted)
    order = onehot(i == wanted + o % R)
    sent = jnp.concatenate([arrived[u] for u in range(NT)], axis=0)
    rows = jnp.dot(order, sent, preferred_element_type=F32).astype(BF16)
    for h in range(NH):
        piece[h] = rows


def regroup_kernel(pieces, grouped):
    x = pieces[...].astype(F32)
    rows = jnp.concatenate(
        [x[ORDER.index(h), s * R : (s + 1) * R] for s in range(KEPT) for h in range(NH)], axis=0
    ).astype(BF16)
    for k in range(NL):
        grouped[k] = rows


def target_kernel(ylo, mine, me, target, *chosen):
    half = target.shape[1] // 2
    n = 2 * NH * NL * R
    k, j = iota((half, n), 0), iota((half, n), 1)
    core, low, high, r = j // 128, (j // 32) % NL, (j // R) % NH, j % R
    column = (high * NL + low) * 64 + (core ^ mine[0]) * 32 + me[0] * R + r
    order = onehot(k == column)
    for dy in range(2):
        start = pl.multiple_of((ylo[0] ^ dy) * half, half)
        got = jnp.dot(
            target[:, pl.ds(start, half)], order, preferred_element_type=F32
        ).astype(BF16)
        for dc in range(2):
            chosen[2 * dy + dc][...] = got[:, dc * 128 : (dc + 1) * 128]


def main_kernel(h, h1, h3, g, g1, g3, weights, t0, t1, t2, t3, o0, o1, o2, o3, gradient):
    hidden = (((h, 0, h, 0), (h1, 0, h3, 4)), ((g, 0, g, 0), (g1, 0, g3, 4)))
    targets, outs = (t0, t1, t2, t3), (o0, o1, o2, o3)

    def tokens(dy, dc, t):
        ref, first = hidden[dc][dy][2 * (t // 4) : 2 * (t // 4) + 2]
        i = t - first
        return jnp.concatenate([ref[i, :TOK], ref[i, TOK : 2 * TOK]], axis=1)

    columns = []
    for t in range(NT):
        halves = [
            jnp.concatenate(
                [weights[k, (2 * t + s) * 32 : (2 * t + s + 1) * 32, :] for k in range(NL)],
                axis=0,
            )
            for s in range(2)
        ]
        columns.append(jnp.concatenate(halves, axis=1))
    residue = []
    for dy in range(2):
        for dc in range(2):
            total = jnp.zeros((TOK, 128), F32)
            for t in range(NT):
                total = total + lax.dot_general(
                    tokens(dy, dc, t),
                    columns[t],
                    (((1,), (1,)), ((), ())),
                    preferred_element_type=F32,
                )
            rounded = total.astype(BF16)
            outs[2 * dy + dc][...] = rounded
            wanted = targets[2 * dy + dc][...]
            residue.append((rounded.astype(F32) - wanted.astype(F32)).astype(BF16))
    for t in range(NT):
        total = jnp.zeros((128, UNITS), F32)
        for dy in range(2):
            for dc in range(2):
                total = total + lax.dot_general(
                    residue[2 * dy + dc],
                    tokens(dy, dc, t),
                    (((0,), (0,)), ((), ())),
                    preferred_element_type=F32,
                )
        total = total.astype(BF16)
        for k in range(NL):
            for s in range(2):
                gradient[k, (2 * t + s) * 32 : (2 * t + s + 1) * 32, :] = total[
                    k * 32 : (k + 1) * 32, s * BLK : (s + 1) * BLK
                ]


def first_sum_kernel(parts, summed):
    total = parts[0].astype(F32)
    for k in range(1, NL):
        total = total + parts[k].astype(F32)
    for h in range(NH):
        summed[ORDER.index(h)] = jnp.concatenate(
            [total[s * 32 + h * R : s * 32 + (h + 1) * R] for s in range(KEPT)], axis=0
        ).astype(BF16)


def spread_kernel(ylo, mine, p0, p1, p2, p3, blocks):
    parts = (p0, p1, p2, p3)
    k, j = iota((512, 512), 0), iota((512, 512), 1)
    x, half, core, odd, low, r = (
        j // 128,
        (j // 64) % 2,
        (j // 32) % 2,
        (j // 16) % 2,
        (j // R) % NL,
        j % R,
    )
    column = low * 32 + (2 * x + odd) * R + r
    order = onehot(k == (half * 2 + (core ^ mine[0])) * 128 + column)
    for dy in range(2):
        rows = jnp.concatenate(
            [
                parts[2 * dy + dc][h * 96 : (h + 1) * 96, :]
                for h in range(2)
                for dc in range(2)
            ],
            axis=1,
        )
        got = jnp.dot(rows, order, preferred_element_type=F32).astype(BF16)
        for i in range(4):
            blocks[4 * (ylo[0] ^ dy) + i] = got[:, i * 128 : (i + 1) * 128]


def second_sum_kernel(parts, blocks, joined):
    total = parts[0].astype(F32)
    for k in range(1, NH):
        total = total + parts[k].astype(F32)
    high = total.astype(BF16).astype(F32)
    low = total - high
    for u in range(NT):
        rows = slice(u * 8, (u + 1) * 8)
        joined[u, :96] = blocks[u]
        joined[u, 96:] = jnp.concatenate([high[rows], low[rows]], axis=0).astype(BF16)


def last_kernel(factor, parts, out, gradient):
    for t in range(NT):
        both = parts[t, 96:].astype(F32)
        rows = (both[:8] + both[8:]) * factor
        for s in range(2):
            gradient[t * R : (t + 1) * R, s * BLK : (s + 1) * BLK] = rows[
                s * R : (s + 1) * R
            ]
    rows = jnp.concatenate([parts[t, :96] for t in range(NT)], axis=1)
    k, j = iota((1024, 512), 0), iota((1024, 512), 1)
    z, core, t, r = j // 64, (j // 32) % 2, (j // R) % NT, j % R
    lane = t * 128 + core * 32 + z * R + r
    for half in range(2):
        order = onehot(k == lane + half * 64)
        out[half * 96 : (half + 1) * 96, :] = jnp.dot(
            rows, order, preferred_element_type=F32
        ).astype(BF16)


def exchange(x, axes, order=None):
    groups = None if order is None else [list(order)]
    return lax.all_to_all(x, axes, 0, 0, axis_index_groups=groups)


def shift(a, y=0, core=0):
    bits = ((y & 1) << 2) | (core << 1) | (y >> 1)
    return lax.ppermute(a, ("ylo", "core", "yhi"), [(i, i ^ bits) for i in range(8)])


def pairs(own, *others):
    return [own] + [shift(a, y=i // 2, core=i % 2) for i, a in enumerate(others, 1)]


def body(teacher, kept, slot, hidden, target):
    place = [lax.axis_index(a).astype(I32)[None] for a in ("ylo", "core", TENSOR)]
    shape = jax.ShapeDtypeStruct
    tile = shape((TOK, 128), BF16)

    packed = call(
        pack_kernel,
        shape((NT, 400, 128), BF16),
        [SMEM, SMEM, VMEM, VMEM],
        kept,
        place[2],
        teacher,
        hidden,
    )
    row = exchange(packed, TENSOR)
    chosen = call(target_kernel, (tile,) * 4, [SMEM] * 3 + [VMEM], *place, target)

    smem = pl.BlockSpec(memory_space=pltpu.SMEM)
    piece = pl.pallas_call(
        compact_kernel,
        out_shape=shape((NH, 64, 128), BF16),
        grid=(1,),
        in_specs=[smem, smem, pl.BlockSpec((NT, 16, 128), lambda i: (0, 24, 0))],
        out_specs=pl.BlockSpec((NH, 64, 128), lambda i: (0, 0, 0)),
        compiler_params=PARAMS,
    )(kept, slot, row)
    pieces = exchange(piece, "zh", ORDER)
    beside = [shift(row[:4], y=1), shift(row[4:], y=3)]
    swapped = shift(row, core=1)
    wanted = pairs(*chosen)
    pieces, swapped, beside, wanted = lax.optimization_barrier((pieces, swapped, beside, wanted))
    grouped = call(regroup_kernel, shape((NL, 512, 128), BF16), [VMEM], pieces)
    weights = exchange(grouped, "zl")
    others = [shift(a, core=1) for a in beside]

    *outs, gradient = call(
        main_kernel,
        (tile,) * 4 + (shape((NL, 512, 128), BF16),),
        [VMEM] * 11,
        row,
        *beside,
        swapped,
        *others,
        weights,
        *wanted,
    )

    parts = exchange(gradient, "zl")
    summed = call(first_sum_kernel, shape((NH, 64, 128), BF16), [VMEM], parts)
    parts = exchange(summed, "zh", ORDER)
    groups = pairs(*outs)
    blocks = call(
        spread_kernel, shape((NT, 96, 128), BF16), [SMEM] * 2 + [VMEM] * 4, *place[:2], *groups
    )
    joined = call(
        second_sum_kernel, shape((NT, 112, 128), BF16), [VMEM, VMEM], parts, blocks
    )
    parts = exchange(joined, TENSOR)
    factor = 1.0 / math.sqrt(TOK * 128)
    student, grad = call(
        lambda *refs: last_kernel(factor, *refs),
        (shape((TOK, 512), BF16), shape((32, UNITS), F32)),
        [VMEM],
        parts,
    )
    return student, grad


def solution(mesh):
    fine = Mesh(np.asarray(mesh.devices).reshape(SIZES), AXES)
    dp = ("ylo", "zh", "zl", "core")
    placed = (P(dp, TENSOR), P(), P(), P(dp, TENSOR), P(dp, None))
    return jax.shard_map(
        body,
        mesh=fine,
        in_specs=placed,
        out_specs=(P(dp, TENSOR), P(dp, TENSOR)),
        check_vma=False,
    )
```

```python
import math

import jax
import jax.numpy as jnp
import numpy as np
from jax import lax
from jax.experimental import pallas as pl
from jax.experimental.pallas import tpu as pltpu
from jax.sharding import Mesh
from jax.sharding import PartitionSpec as P

BF16 = jnp.bfloat16
F32 = jnp.float32
I32 = jnp.int32

AXES = ("ylo", "zh", "zl", "core", "yhi", "x")
SIZES = (2, 8, 4, 2, 2, 4)
TENSOR = ("yhi", "x")

BLK = 128
KEPT = 16
MOST = 4
NT = 8
NH = 8
NL = 4
GATHER = tuple((h + 5) % NH for h in range(NH))
SCATTER = tuple((h + 4) % NH for h in range(NH))
R = 4
SHARD = 28
TOK = 192
UNITS = 256

VMEM = pl.BlockSpec(memory_space=pltpu.VMEM)
SMEM = pl.BlockSpec(memory_space=pltpu.SMEM)
PARAMS = pltpu.CompilerParams(vmem_limit_bytes=40 * 1024 * 1024)
WHOLE = pltpu.CompilerParams(vmem_limit_bytes=60 * 1024 * 1024)


def iota(shape, axis):
    return lax.broadcasted_iota(I32, shape, axis)


def onehot(mask):
    return jnp.where(mask, 1.0, 0.0).astype(BF16)


def call(kernel, out, specs, *args, params=PARAMS):
    return pl.pallas_call(
        kernel,
        out_shape=out,
        in_specs=specs,
        out_specs=jax.tree.map(lambda _: VMEM, out),
        compiler_params=params,
    )(*args)


def pack_kernel(kept, me, teacher, hidden, packed):
    base = me[0] * SHARD
    count = jnp.int32(0)
    places = [jnp.int32(0)] * MOST
    for j in range(KEPT):
        within = kept[j] - base
        mine = (within >= 0) & (within < SHARD)
        for p in range(MOST):
            places[p] = jnp.where(mine & (count == p), within, places[p])
        count = count + mine.astype(I32)
    rows = NT * R
    picked = jnp.concatenate(
        [teacher[:, pl.ds(pl.multiple_of(w * BLK, BLK), BLK)] for w in places], axis=0
    )
    n = MOST * rows
    o, i = iota((n, n), 0), iota((n, n), 1)
    t, p, r = o // (MOST * R), (o // R) % MOST, o % R
    order = onehot(i == p * rows + t * R + r)
    blocks = jnp.dot(order, picked, preferred_element_type=F32).astype(BF16)
    for m in range(NT):
        packed[m, :TOK] = hidden[:, :BLK]
        packed[m, TOK : 2 * TOK] = hidden[:, BLK:]
        packed[m, 2 * TOK :] = blocks[m * 16 : (m + 1) * 16]


def compact_kernel(kept, slot, arrived, piece):
    n, m = KEPT * R, NT * MOST * R
    o, i = iota((n, m), 0), iota((n, m), 1)
    shard = [(kept[j] * 2341) >> 16 for j in range(KEPT)]
    wanted = jnp.zeros((n, m), I32)
    for j in range(KEPT):
        place = jnp.int32(0)
        for k in range(j):
            place = place + (shard[k] == shard[j]).astype(I32)
        wanted = jnp.where(o // R == slot[j], (shard[j] * MOST + place) * R, wanted)
    order = onehot(i == wanted + o % R)
    sent = jnp.concatenate([arrived[u] for u in range(NT)], axis=0)
    rows = jnp.dot(order, sent, preferred_element_type=F32).astype(BF16)
    for h in range(NH):
        piece[h] = rows


def regroup_kernel(pieces, grouped):
    x = pieces[...].astype(F32)
    rows = jnp.concatenate(
        [x[GATHER.index(h), s * R : (s + 1) * R] for s in range(KEPT) for h in range(NH)], axis=0
    ).astype(BF16)
    for k in range(NL):
        grouped[k] = rows


def target_kernel(ylo, mine, me, target, *chosen):
    half = target.shape[1] // 2
    n = 2 * NH * NL * R
    k, j = iota((half, n), 0), iota((half, n), 1)
    core, low, high, r = j // 128, (j // 32) % NL, (j // R) % NH, j % R
    column = (high * NL + low) * 64 + (core ^ mine[0]) * 32 + me[0] * R + r
    order = onehot(k == column)
    for dy in range(2):
        start = pl.multiple_of((ylo[0] ^ dy) * half, half)
        got = jnp.dot(
            target[:, pl.ds(start, half)], order, preferred_element_type=F32
        ).astype(BF16)
        for dc in range(2):
            chosen[2 * dy + dc][...] = got[:, dc * 128 : (dc + 1) * 128]


def main_kernel(h, h1, h3, g, g1, g3, weights, t0, t1, t2, t3, o0, o1, o2, o3, gradient):
    hidden = (((h, 0, h, 0), (h1, 0, h3, 4)), ((g, 0, g, 0), (g1, 0, g3, 4)))
    targets, outs = (t0, t1, t2, t3), (o0, o1, o2, o3)

    def tokens(dy, dc, t):
        ref, first = hidden[dc][dy][2 * (t // 4) : 2 * (t // 4) + 2]
        i = t - first
        return jnp.concatenate([ref[i, :TOK], ref[i, TOK : 2 * TOK]], axis=1)

    columns = []
    for t in range(NT):
        halves = [
            jnp.concatenate(
                [weights[k, (2 * t + s) * 32 : (2 * t + s + 1) * 32, :] for k in range(NL)],
                axis=0,
            )
            for s in range(2)
        ]
        columns.append(jnp.concatenate(halves, axis=1))
    residue = []
    for dy in range(2):
        for dc in range(2):
            total = jnp.zeros((TOK, 128), F32)
            for t in range(NT):
                total = total + lax.dot_general(
                    tokens(dy, dc, t),
                    columns[t],
                    (((1,), (1,)), ((), ())),
                    preferred_element_type=F32,
                )
            rounded = total.astype(BF16)
            outs[2 * dy + dc][...] = rounded
            wanted = targets[2 * dy + dc][...]
            residue.append((rounded.astype(F32) - wanted.astype(F32)).astype(BF16))
    for t in range(NT):
        total = jnp.zeros((128, UNITS), F32)
        for dy in range(2):
            for dc in range(2):
                total = total + lax.dot_general(
                    residue[2 * dy + dc],
                    tokens(dy, dc, t),
                    (((0,), (0,)), ((), ())),
                    preferred_element_type=F32,
                )
        total = total.astype(BF16)
        for k in range(NL):
            for s in range(2):
                gradient[k, (2 * t + s) * 32 : (2 * t + s + 1) * 32, :] = total[
                    k * 32 : (k + 1) * 32, s * BLK : (s + 1) * BLK
                ]


def first_sum_kernel(parts, summed):
    total = parts[0].astype(F32)
    for k in range(1, NL):
        total = total + parts[k].astype(F32)
    for h in range(NH):
        summed[SCATTER.index(h)] = jnp.concatenate(
            [total[s * 32 + h * R : s * 32 + (h + 1) * R] for s in range(KEPT)], axis=0
        ).astype(BF16)


def spread_kernel(ylo, mine, p0, p1, p2, p3, blocks):
    parts = (p0, p1, p2, p3)
    k, j = iota((512, 512), 0), iota((512, 512), 1)
    x, half, core, odd, low, r = (
        j // 128,
        (j // 64) % 2,
        (j // 32) % 2,
        (j // 16) % 2,
        (j // R) % NL,
        j % R,
    )
    column = low * 32 + (2 * x + odd) * R + r
    order = onehot(k == (half * 2 + (core ^ mine[0])) * 128 + column)
    for dy in range(2):
        rows = jnp.concatenate(
            [
                parts[2 * dy + dc][h * 96 : (h + 1) * 96, :]
                for h in range(2)
                for dc in range(2)
            ],
            axis=1,
        )
        got = jnp.dot(rows, order, preferred_element_type=F32).astype(BF16)
        for i in range(4):
            blocks[4 * (ylo[0] ^ dy) + i] = got[:, i * 128 : (i + 1) * 128]


def second_sum_kernel(parts, blocks, joined):
    total = parts[0].astype(F32)
    for k in range(1, NH):
        total = total + parts[k].astype(F32)
    high = total.astype(BF16).astype(F32)
    low = total - high
    for u in range(NT):
        rows = slice(u * 8, (u + 1) * 8)
        joined[u, :96] = blocks[u]
        joined[u, 96:] = jnp.concatenate([high[rows], low[rows]], axis=0).astype(BF16)


def last_kernel(factor, parts, out, gradient):
    for t in range(NT):
        both = parts[t, 96:].astype(F32)
        rows = (both[:8] + both[8:]) * factor
        for s in range(2):
            gradient[t * R : (t + 1) * R, s * BLK : (s + 1) * BLK] = rows[
                s * R : (s + 1) * R
            ]
    rows = jnp.concatenate([parts[t, :96] for t in range(NT)], axis=1)
    k, j = iota((1024, 512), 0), iota((1024, 512), 1)
    z, core, t, r = j // 64, (j // 32) % 2, (j // R) % NT, j % R
    lane = t * 128 + core * 32 + z * R + r
    for half in range(2):
        order = onehot(k == lane + half * 64)
        out[half * 96 : (half + 1) * 96, :] = jnp.dot(
            rows, order, preferred_element_type=F32
        ).astype(BF16)


def exchange(x, axes, order=None):
    groups = None if order is None else [list(order)]
    return lax.all_to_all(x, axes, 0, 0, axis_index_groups=groups)


def exchange_near(x):
    groups = []
    for start in range(0, NH * NL, NL):
        for core in range(2):
            members = [(start + 2 * core + i) % (NH * NL) for i in range(NL)]
            groups.append([2 * z + core for z in sorted(members, key=lambda z: z % NL)])
    return lax.all_to_all(x, ("zh", "zl", "core"), 0, 0, axis_index_groups=groups)


def shift(a, y=0, core=0):
    bits = ((y & 1) << 2) | (core << 1) | (y >> 1)
    return lax.ppermute(a, ("ylo", "core", "yhi"), [(i, i ^ bits) for i in range(8)])


def pairs(own, *others):
    return [own] + [shift(a, y=i // 2, core=i % 2) for i, a in enumerate(others, 1)]


def body(teacher, kept, slot, hidden, target):
    place = [lax.axis_index(a).astype(I32)[None] for a in ("ylo", "core", TENSOR)]
    shape = jax.ShapeDtypeStruct
    tile = shape((TOK, 128), BF16)

    packed = call(
        pack_kernel,
        shape((NT, 400, 128), BF16),
        [SMEM, SMEM, VMEM, VMEM],
        kept,
        place[2],
        teacher,
        hidden,
        params=WHOLE,
    )
    row = exchange(packed, TENSOR)
    chosen = call(target_kernel, (tile,) * 4, [SMEM] * 3 + [VMEM], *place, target)
    targets = pairs(*chosen)
    row, targets = lax.optimization_barrier((row, targets))

    smem = pl.BlockSpec(memory_space=pltpu.SMEM)
    piece = pl.pallas_call(
        compact_kernel,
        out_shape=shape((NH, 64, 128), BF16),
        grid=(1,),
        in_specs=[smem, smem, pl.BlockSpec((NT, 16, 128), lambda i: (0, 24, 0))],
        out_specs=pl.BlockSpec((NH, 64, 128), lambda i: (0, 0, 0)),
        compiler_params=PARAMS,
    )(kept, slot, row)
    pieces = exchange(piece, "zh", GATHER)
    beside = [shift(row[:4], y=1), shift(row[4:], y=3)]
    pieces, beside = lax.optimization_barrier((pieces, beside))
    grouped = call(regroup_kernel, shape((NL, 512, 128), BF16), [VMEM], pieces)
    weights = exchange_near(grouped)
    others = [shift(a, core=1) for a in (row, *beside)]

    *outs, gradient = call(
        main_kernel,
        (tile,) * 4 + (shape((NL, 512, 128), BF16),),
        [VMEM] * 11,
        row,
        *beside,
        *others,
        weights,
        *targets,
    )

    parts = exchange_near(gradient)
    summed = call(first_sum_kernel, shape((NH, 64, 128), BF16), [VMEM], parts)
    parts = exchange(summed, "zh", SCATTER)
    groups = pairs(*outs)
    blocks = call(
        spread_kernel, shape((NT, 96, 128), BF16), [SMEM] * 2 + [VMEM] * 4, *place[:2], *groups
    )
    joined = call(
        second_sum_kernel, shape((NT, 112, 128), BF16), [VMEM, VMEM], parts, blocks
    )
    parts = exchange(joined, TENSOR)
    factor = 1.0 / math.sqrt(TOK * 128)
    student, grad = call(
        lambda *refs: last_kernel(factor, *refs),
        (shape((TOK, 512), BF16), shape((32, UNITS), F32)),
        [VMEM],
        parts,
    )
    return student, grad


def solution(mesh):
    fine = Mesh(np.asarray(mesh.devices).reshape(SIZES), AXES)
    dp = ("ylo", "zh", "zl", "core")
    placed = (P(dp, TENSOR), P(), P(), P(dp, TENSOR), P(dp, None))
    return jax.shard_map(
        body,
        mesh=fine,
        in_specs=placed,
        out_specs=(P(dp, TENSOR), P(dp, TENSOR)),
        check_vma=False,
    )
```

```python
import math

import jax
import jax.numpy as jnp
import numpy as np
from jax import lax
from jax.experimental import pallas as pl
from jax.experimental.pallas import tpu as pltpu
from jax.sharding import Mesh
from jax.sharding import PartitionSpec as P

BF16 = jnp.bfloat16
F32 = jnp.float32
I32 = jnp.int32

AXES = ("ylo", "zh", "zl", "core", "yhi", "x")
SIZES = (2, 8, 4, 2, 2, 4)
TENSOR = ("yhi", "x")

BLK = 128
KEPT = 16
MOST = 4
NT = 8
NH = 8
NL = 4
GATHER = tuple((h + 5) % NH for h in range(NH))
SCATTER = tuple((h + 4) % NH for h in range(NH))
R = 4
SHARD = 28
TOK = 192
UNITS = 256

VMEM = pl.BlockSpec(memory_space=pltpu.VMEM)
SMEM = pl.BlockSpec(memory_space=pltpu.SMEM)
PARAMS = pltpu.CompilerParams(vmem_limit_bytes=40 * 1024 * 1024)
WHOLE = pltpu.CompilerParams(vmem_limit_bytes=60 * 1024 * 1024)


def iota(shape, axis):
    return lax.broadcasted_iota(I32, shape, axis)


def onehot(mask):
    return jnp.where(mask, 1.0, 0.0).astype(BF16)


def call(kernel, out, specs, *args, params=PARAMS):
    return pl.pallas_call(
        kernel,
        out_shape=out,
        in_specs=specs,
        out_specs=jax.tree.map(lambda _: VMEM, out),
        compiler_params=params,
    )(*args)


def pack_kernel(kept, me, teacher, hidden, packed):
    base = me[0] * SHARD
    count = jnp.int32(0)
    places = [jnp.int32(0)] * MOST
    for j in range(KEPT):
        within = kept[j] - base
        mine = (within >= 0) & (within < SHARD)
        for p in range(MOST):
            places[p] = jnp.where(mine & (count == p), within, places[p])
        count = count + mine.astype(I32)
    rows = NT * R
    picked = jnp.concatenate(
        [teacher[:, pl.ds(pl.multiple_of(w * BLK, BLK), BLK)] for w in places], axis=0
    )
    n = MOST * rows
    o, i = iota((n, n), 0), iota((n, n), 1)
    t, p, r = o // (MOST * R), (o // R) % MOST, o % R
    order = onehot(i == p * rows + t * R + r)
    blocks = jnp.dot(order, picked, preferred_element_type=F32).astype(BF16)
    for m in range(NT):
        packed[m, :TOK] = hidden[:, :BLK]
        packed[m, TOK : 2 * TOK] = hidden[:, BLK:]
        packed[m, 2 * TOK :] = blocks[m * 16 : (m + 1) * 16]


def compact_kernel(kept, slot, arrived, piece):
    n, m = KEPT * R, NT * MOST * R
    o, i = iota((n, m), 0), iota((n, m), 1)
    shard = [(kept[j] * 2341) >> 16 for j in range(KEPT)]
    wanted = jnp.zeros((n, m), I32)
    for j in range(KEPT):
        place = jnp.int32(0)
        for k in range(j):
            place = place + (shard[k] == shard[j]).astype(I32)
        wanted = jnp.where(o // R == slot[j], (shard[j] * MOST + place) * R, wanted)
    order = onehot(i == wanted + o % R)
    sent = jnp.concatenate([arrived[u] for u in range(NT)], axis=0)
    rows = jnp.dot(order, sent, preferred_element_type=F32).astype(BF16)
    for h in range(NH):
        piece[h] = rows


def regroup_kernel(pieces, grouped):
    x = pieces[...].astype(F32)
    rows = jnp.concatenate(
        [x[GATHER.index(h), s * R : (s + 1) * R] for s in range(KEPT) for h in range(NH)], axis=0
    ).astype(BF16)
    for k in range(NL):
        grouped[k] = rows


def target_kernel(ylo, mine, me, target, *chosen):
    half = target.shape[1] // 2
    n = 2 * NH * NL * R
    k, j = iota((half, n), 0), iota((half, n), 1)
    core, low, high, r = j // 128, (j // 32) % NL, (j // R) % NH, j % R
    column = (high * NL + low) * 64 + (core ^ mine[0]) * 32 + me[0] * R + r
    order = onehot(k == column)
    for dy in range(2):
        start = pl.multiple_of((ylo[0] ^ dy) * half, half)
        got = jnp.dot(
            target[:, pl.ds(start, half)], order, preferred_element_type=F32
        ).astype(BF16)
        for dc in range(2):
            chosen[2 * dy + dc][...] = got[:, dc * 128 : (dc + 1) * 128]


def main_kernel(h, h1, h3, g, g1, g3, weights, t0, t1, t2, t3, o0, o1, o2, o3, gradient):
    hidden = (((h, 0, h, 0), (h1, 0, h3, 4)), ((g, 0, g, 0), (g1, 0, g3, 4)))
    targets, outs = (t0, t1, t2, t3), (o0, o1, o2, o3)

    def tokens(dy, dc, t):
        ref, first = hidden[dc][dy][2 * (t // 4) : 2 * (t // 4) + 2]
        i = t - first
        return jnp.concatenate([ref[i, :TOK], ref[i, TOK : 2 * TOK]], axis=1)

    columns = []
    for t in range(NT):
        halves = [
            jnp.concatenate(
                [weights[k, (2 * t + s) * 32 : (2 * t + s + 1) * 32, :] for k in range(NL)],
                axis=0,
            )
            for s in range(2)
        ]
        columns.append(jnp.concatenate(halves, axis=1))
    residue = []
    for dy in range(2):
        for dc in range(2):
            total = jnp.zeros((TOK, 128), F32)
            for t in range(NT):
                total = total + lax.dot_general(
                    tokens(dy, dc, t),
                    columns[t],
                    (((1,), (1,)), ((), ())),
                    preferred_element_type=F32,
                )
            rounded = total.astype(BF16)
            outs[2 * dy + dc][...] = rounded
            wanted = targets[2 * dy + dc][...]
            residue.append((rounded.astype(F32) - wanted.astype(F32)).astype(BF16))
    for t in range(NT):
        total = jnp.zeros((128, UNITS), F32)
        for dy in range(2):
            for dc in range(2):
                total = total + lax.dot_general(
                    residue[2 * dy + dc],
                    tokens(dy, dc, t),
                    (((0,), (0,)), ((), ())),
                    preferred_element_type=F32,
                )
        total = total.astype(BF16)
        for k in range(NL):
            for s in range(2):
                gradient[k, (2 * t + s) * 32 : (2 * t + s + 1) * 32, :] = total[
                    k * 32 : (k + 1) * 32, s * BLK : (s + 1) * BLK
                ]


def first_sum_kernel(parts, summed):
    total = parts[0].astype(F32)
    for k in range(1, NL):
        total = total + parts[k].astype(F32)
    for h in range(NH):
        summed[SCATTER.index(h)] = jnp.concatenate(
            [total[s * 32 + h * R : s * 32 + (h + 1) * R] for s in range(KEPT)], axis=0
        ).astype(BF16)


def spread_kernel(ylo, mine, p0, p1, p2, p3, blocks):
    parts = (p0, p1, p2, p3)
    k, j = iota((512, 512), 0), iota((512, 512), 1)
    x, half, core, odd, low, r = (
        j // 128,
        (j // 64) % 2,
        (j // 32) % 2,
        (j // 16) % 2,
        (j // R) % NL,
        j % R,
    )
    column = low * 32 + (2 * x + odd) * R + r
    order = onehot(k == (half * 2 + (core ^ mine[0])) * 128 + column)
    for dy in range(2):
        rows = jnp.concatenate(
            [
                parts[2 * dy + dc][h * 96 : (h + 1) * 96, :]
                for h in range(2)
                for dc in range(2)
            ],
            axis=1,
        )
        got = jnp.dot(rows, order, preferred_element_type=F32).astype(BF16)
        for i in range(4):
            blocks[4 * (ylo[0] ^ dy) + i] = got[:, i * 128 : (i + 1) * 128]


def second_sum_kernel(parts, blocks, joined):
    total = parts[0].astype(F32)
    for k in range(1, NH):
        total = total + parts[k].astype(F32)
    high = total.astype(BF16).astype(F32)
    low = total - high
    for u in range(NT):
        rows = slice(u * 8, (u + 1) * 8)
        joined[u, :96] = blocks[u]
        joined[u, 96:] = jnp.concatenate([high[rows], low[rows]], axis=0).astype(BF16)


def last_kernel(factor, parts, out, gradient):
    for t in range(NT):
        both = parts[t, 96:].astype(F32)
        rows = (both[:8] + both[8:]) * factor
        for s in range(2):
            gradient[t * R : (t + 1) * R, s * BLK : (s + 1) * BLK] = rows[
                s * R : (s + 1) * R
            ]
    rows = jnp.concatenate([parts[t, :96] for t in range(NT)], axis=1)
    k, j = iota((1024, 512), 0), iota((1024, 512), 1)
    z, core, t, r = j // 64, (j // 32) % 2, (j // R) % NT, j % R
    lane = t * 128 + core * 32 + z * R + r
    for half in range(2):
        order = onehot(k == lane + half * 64)
        out[half * 96 : (half + 1) * 96, :] = jnp.dot(
            rows, order, preferred_element_type=F32
        ).astype(BF16)


def exchange(x, axes, order=None):
    groups = None if order is None else [list(order)]
    return lax.all_to_all(x, axes, 0, 0, axis_index_groups=groups)


def exchange_near(x):
    groups = []
    for start in range(0, NH * NL, NL):
        for core in range(2):
            members = [(start + 2 * core + i) % (NH * NL) for i in range(NL)]
            groups.append([2 * z + core for z in sorted(members, key=lambda z: z % NL)])
    return lax.all_to_all(x, ("zh", "zl", "core"), 0, 0, axis_index_groups=groups)


def shift(a, y=0, core=0):
    bits = ((y & 1) << 2) | (core << 1) | (y >> 1)
    return lax.ppermute(a, ("ylo", "core", "yhi"), [(i, i ^ bits) for i in range(8)])


def pairs(own, *others):
    return [own] + [shift(a, y=i // 2, core=i % 2) for i, a in enumerate(others, 1)]


def body(teacher, kept, slot, hidden, target):
    place = [lax.axis_index(a).astype(I32)[None] for a in ("ylo", "core", TENSOR)]
    shape = jax.ShapeDtypeStruct
    tile = shape((TOK, 128), BF16)

    packed = call(
        pack_kernel,
        shape((NT, 400, 128), BF16),
        [SMEM, SMEM, VMEM, VMEM],
        kept,
        place[2],
        teacher,
        hidden,
        params=WHOLE,
    )
    row = exchange(packed, TENSOR)
    chosen = call(target_kernel, (tile,) * 4, [SMEM] * 3 + [VMEM], *place, target)
    targets = pairs(*chosen)
    row, targets = lax.optimization_barrier((row, targets))

    smem = pl.BlockSpec(memory_space=pltpu.SMEM)
    piece = pl.pallas_call(
        compact_kernel,
        out_shape=shape((NH, 64, 128), BF16),
        grid=(1,),
        in_specs=[smem, smem, pl.BlockSpec((NT, 16, 128), lambda i: (0, 24, 0))],
        out_specs=pl.BlockSpec((NH, 64, 128), lambda i: (0, 0, 0)),
        compiler_params=PARAMS,
    )(kept, slot, row)
    pieces = exchange(piece, "zh", GATHER)
    beside = [shift(row[:4, : 2 * TOK], y=1), shift(row[4:, : 2 * TOK], y=3)]
    pieces, beside = lax.optimization_barrier((pieces, beside))
    grouped = call(regroup_kernel, shape((NL, 512, 128), BF16), [VMEM], pieces)
    weights = exchange_near(grouped)
    others = [shift(a, core=1) for a in (row, *beside)]

    *outs, gradient = call(
        main_kernel,
        (tile,) * 4 + (shape((NL, 512, 128), BF16),),
        [VMEM] * 11,
        row,
        *beside,
        *others,
        weights,
        *targets,
        params=WHOLE,
    )

    parts = exchange_near(gradient)
    near = shift(outs[1], core=1)
    parts, near = lax.optimization_barrier((parts, near))
    summed = call(first_sum_kernel, shape((NH, 64, 128), BF16), [VMEM], parts)
    parts = exchange(summed, "zh", SCATTER)
    groups = [outs[0], near, shift(outs[2], y=1), shift(outs[3], y=1, core=1)]
    blocks = call(
        spread_kernel, shape((NT, 96, 128), BF16), [SMEM] * 2 + [VMEM] * 4, *place[:2], *groups
    )
    joined = call(
        second_sum_kernel, shape((NT, 112, 128), BF16), [VMEM, VMEM], parts, blocks
    )
    parts = exchange(joined, TENSOR)
    factor = 1.0 / math.sqrt(TOK * 128)
    student, grad = call(
        lambda *refs: last_kernel(factor, *refs),
        (shape((TOK, 512), BF16), shape((32, UNITS), F32)),
        [VMEM],
        parts,
    )
    return student, grad


def solution(mesh):
    fine = Mesh(np.asarray(mesh.devices).reshape(SIZES), AXES)
    dp = ("ylo", "zh", "zl", "core")
    placed = (P(dp, TENSOR), P(), P(), P(dp, TENSOR), P(dp, None))
    return jax.shard_map(
        body,
        mesh=fine,
        in_specs=placed,
        out_specs=(P(dp, TENSOR), P(dp, TENSOR)),
        check_vma=False,
    )
```
